32 devices in a mesh: groups: 2 (over x), tile: 16 (over z, y, core).
Axes of the slice: x: 2, y: 2, z: 4, core: 2. Of those that a mesh axis runs over, the one named last changes fastest.
Arguments:
- object_tiles: float32 [32, 2, 768, 768], P(('groups', 'tile')), parts along dimension 0, may hold values from -6 to 6
- probe: float32 [2, 256, 256], replicated, may hold values from -6 to 6
- intensity: bfloat16 [1024, 256, 256], P(('groups', 'tile')), parts along dimension 0, may hold values from 0 to 8
- counts: int32 [32], P(('groups', 'tile')), parts along dimension 0, may hold values from 1 to 32, 256 in all
- offsets: int32 [1024, 2], P(('groups', 'tile')), parts along dimension 0, may hold values from 0 to 767, as said below
Outputs:
- object_new: float32 [32, 2, 768, 768], P(('groups', 'tile')), parts along dimension 0
- probe_step: float32 [4, 256, 256], P('groups'), parts along dimension 0
The draws below stay inside these ranges and needn't reach their ends.
There are 2 independent parts, one for each index of `groups`. The reference program is written for one: setup_inputs(seed, part) draws one part's arguments, and reference() takes and returns one part's arrays. A program takes and returns all parts, laid end to end along the dimension named above; an argument that names none is the same for every part. Nothing has to cross between parts.
Inputs may be any that keep to these rules, and one draw needn't show every extreme that they name: `counts`: live patterns of a tile; some tile has exactly 32. `offsets`: pixel offset of a window within its tile; 767 occurs in every draw.
All inputs are finite; a program needn't handle non-finite values. No bound on the sum of `counts` on one device may be relied on, other than what follows from the above.
Results may differ from the reference program's by a relative error of at most 0.0049.
Values sent between devices are 32-bit elements; how exact they have to be, the bound alone decides.
A program may use at most 192 MiB of HBM per device.

```python
import math
import jax
import jax.numpy as jnp
import numpy as np
from jax import lax

PROBE_SIDE = 256
TILE_SIDE = 768
PATTERN_SLOTS = 32
TILES = 16
PATTERNS = 512
N_TILE = 16


def draw_offsets(key, part):
    key = jax.random.fold_in(key, 7)
    first_key, second_key = jax.random.split(key)
    values = jax.random.randint(first_key, (PATTERNS, 2), 0, TILE_SIDE)
    chosen = jax.random.randint(second_key, (), 0, PATTERNS)
    row_ids = jnp.arange(PATTERNS)[:, None]
    return jnp.where(row_ids == chosen, TILE_SIDE - 1, values).astype(jnp.int32)


def block_levels(key, shape, cuts, smallest, high):
    gain = 1.0
    for position, blocks in cuts:
        draws = jax.random.uniform(jax.random.fold_in(jax.random.fold_in(key, 6), position), (blocks,), jnp.float32, smallest / len(cuts), high / len(cuts))
        gain = gain * jnp.repeat(jnp.exp(draws), shape[position] // blocks).reshape((-1,) + (1,) * (len(shape) - 1 - position))
    return gain


def profile(amount, total, limit, skew):
    portions = [(1 << 20) // math.isqrt(rank ** skew) + 1 for rank in range(2, amount + 1)]
    surplus, given = total - limit - (amount - 1), [1] * (amount - 1)
    while surplus > 0:
        movable = [i for i in range(amount - 1) if given[i] < limit]
        pool, left = sum([portions[i] for i in movable]), surplus
        for i in movable:
            more = min(limit - given[i], max(1, left * portions[i] // pool), surplus)
            given[i] = given[i] + more
            surplus = surplus - more
    return np.array([limit] + given)


def ragged(stream_key, number_of, total, limit, skew):
    if number_of == 2:
        one = jax.random.randint(stream_key, (), max(1, total - limit), min(limit, total - 1) + 1)
        return jnp.stack([one, total - one])
    sizes = jnp.asarray(profile(number_of, total, limit, skew), jnp.int32)
    twos = (number_of - 1) // 2
    donor, taker = sizes[1:1 + 2 * twos:2], sizes[2:2 + 2 * twos:2]
    room = jnp.minimum(donor - 1, limit - taker)
    moved = jax.random.randint(jax.random.fold_in(stream_key, 1), (twos,), 0, 1 << 20) % (room + 1)
    sizes = sizes.at[1:1 + 2 * twos:2].set(donor - moved).at[2:2 + 2 * twos:2].set(taker + moved)
    return sizes[jax.random.permutation(jax.random.fold_in(stream_key, 2), number_of)]


def scatter_about(stream_key, extent, deviation, reach, cuts=(), kind=jnp.bfloat16):
    loudness = block_levels(stream_key, extent, cuts, -0.22, 0.18) if cuts else 1.0
    values = jax.random.normal(stream_key, extent, jnp.float32) * deviation * loudness
    return jnp.minimum(jnp.maximum(values, -reach), reach).astype(kind)


def setup_inputs(seed: int = 0, part: int = 0) -> dict:
    key_of = jax.random.split(jax.random.key(seed), 6)
    part_splits = jax.random.split(jax.random.fold_in(key_of[5], part), 6)
    object_tiles = scatter_about(part_splits[0], (TILES, 2, TILE_SIDE, TILE_SIDE), 1.0, 6.0, ((0, 16),), jnp.float32)
    probe = scatter_about(key_of[1], (2, PROBE_SIDE, PROBE_SIDE), 1.0, 6.0, (), jnp.float32)
    intensity = jnp.clip(8.0 * jax.random.uniform(part_splits[2], (PATTERNS, PROBE_SIDE, PROBE_SIDE), jnp.float32) ** block_levels(part_splits[2], (PATTERNS, PROBE_SIDE, PROBE_SIDE), ((0, 16),), -0.2, 0.2), 0.0, 8.0).astype(jnp.bfloat16)
    counts = ragged(part_splits[3], TILES, TILES * PATTERN_SLOTS // 2, PATTERN_SLOTS, 2).astype(jnp.int32)
    offsets = draw_offsets(jax.random.fold_in(jax.random.fold_in(key_of[5], part), 71), part)
    return {"object_tiles": object_tiles, "probe": probe, "intensity": intensity, "counts": counts, "offsets": offsets}


floor_amp = 0.5
object_damp = 0.5
probe_damp = 1.0

def dft_tables():
    steps = jnp.arange(PROBE_SIDE, dtype=jnp.int32)
    phase = steps[:, None] * steps[None, :] % PROBE_SIDE
    angle = phase.astype(jnp.float32) * (2.0 * math.pi / PROBE_SIDE)
    scale = 1.0 / math.sqrt(PROBE_SIDE)
    return ((jnp.cos(angle) * scale).astype(jnp.bfloat16), (-jnp.sin(angle) * scale).astype(jnp.bfloat16))

def apply_left(matrix, batch):
    return jnp.einsum('ab,jbc->jac', matrix.astype(jnp.float32), batch.astype(jnp.float32))

def apply_right(batch, matrix):
    return jnp.einsum('jab,bc->jac', batch.astype(jnp.float32), matrix.astype(jnp.float32))

def correction(patch_re, patch_im, probe_re, probe_im, measured, live_mask, table_re, table_im):
    exit_re = (probe_re * patch_re - probe_im * patch_im).astype(jnp.bfloat16)
    exit_im = (probe_re * patch_im + probe_im * patch_re).astype(jnp.bfloat16)
    half_re = (apply_left(table_re, exit_re) - apply_left(table_im, exit_im)).astype(jnp.bfloat16)
    half_im = (apply_left(table_re, exit_im) + apply_left(table_im, exit_re)).astype(jnp.bfloat16)
    far_re = apply_right(half_re, table_re) - apply_right(half_im, table_im)
    far_im = apply_right(half_re, table_im) + apply_right(half_im, table_re)
    modulus = jnp.sqrt(far_re * far_re + far_im * far_im)
    factor = live_mask * (jnp.sqrt(measured.astype(jnp.float32)) / jnp.maximum(modulus, floor_amp) - 1.0)
    diff_re = (far_re * factor).astype(jnp.bfloat16)
    diff_im = (far_im * factor).astype(jnp.bfloat16)
    back_re = (apply_left(table_re, diff_re) + apply_left(table_im, diff_im)).astype(jnp.bfloat16)
    back_im = (apply_left(table_re, diff_im) - apply_left(table_im, diff_re)).astype(jnp.bfloat16)
    chi_re = apply_right(back_re, table_re) + apply_right(back_im, table_im)
    chi_im = apply_right(back_im, table_re) - apply_right(back_re, table_im)
    return (chi_re, chi_im)

def reference(object_tiles, probe, intensity, counts, offsets):
    grid_cols = N_TILE // 2
    image = object_tiles.reshape(2, grid_cols, 2, TILE_SIDE, TILE_SIDE).transpose(2, 0, 3, 1, 4)
    image = image.reshape(2, 2 * TILE_SIDE, grid_cols * TILE_SIDE)
    padded = jnp.pad(image, ((0, 0), (0, PROBE_SIDE), (0, PROBE_SIDE)))
    table_re, table_im = dft_tables()
    probe_re = probe[0]
    probe_im = probe[1]
    zero_at = jnp.zeros((), jnp.int32)

    def per_tile(carry, items):
        gradient, probe_sums = carry
        tile_id, tile_int, tile_off, tile_count = items
        row_start = (tile_id // grid_cols * TILE_SIDE + tile_off[:, 0]).astype(jnp.int32)
        col_start = (tile_id % grid_cols * TILE_SIDE + tile_off[:, 1]).astype(jnp.int32)

        def window_at(row_at, col_at):
            return lax.dynamic_slice(padded, (zero_at, row_at, col_at), (2, PROBE_SIDE, PROBE_SIDE))
        patches = jax.vmap(window_at)(row_start, col_start)
        patch_re = patches[:, 0]
        patch_im = patches[:, 1]
        live_mask = (jnp.arange(PATTERN_SLOTS, dtype=jnp.int32) < tile_count).astype(jnp.float32)[:, None, None]
        chi_re, chi_im = correction(patch_re, patch_im, probe_re, probe_im, tile_int, live_mask, table_re, table_im)
        pieces = jnp.stack([probe_re * chi_re + probe_im * chi_im, probe_re * chi_im - probe_im * chi_re, live_mask * (probe_re * probe_re + probe_im * probe_im)[None]], axis=1)

        def add_piece(slot, grad_now):
            row_at = row_start[slot]
            col_at = col_start[slot]
            current = lax.dynamic_slice(grad_now, (zero_at, row_at, col_at), (3, PROBE_SIDE, PROBE_SIDE))
            return lax.dynamic_update_slice(grad_now, current + pieces[slot], (zero_at, row_at, col_at))
        gradient = lax.fori_loop(0, PATTERN_SLOTS, add_piece, gradient)
        sums_here = jnp.stack([lax.optimization_barrier(jnp.sum(patch_re * chi_re + patch_im * chi_im, axis=0)), lax.optimization_barrier(jnp.sum(patch_re * chi_im - patch_im * chi_re, axis=0)), lax.optimization_barrier(jnp.sum(live_mask * (patch_re * patch_re + patch_im * patch_im), axis=0))])
        return ((gradient, probe_sums + sums_here), None)
    start_grad = jnp.zeros((3, 2 * TILE_SIDE + PROBE_SIDE, grid_cols * TILE_SIDE + PROBE_SIDE), jnp.float32)
    start_probe = jnp.zeros((3, PROBE_SIDE, PROBE_SIDE), jnp.float32)
    items = (jnp.arange(TILES, dtype=jnp.int32), intensity.reshape(TILES, PATTERN_SLOTS, PROBE_SIDE, PROBE_SIDE), offsets.reshape(TILES, PATTERN_SLOTS, 2), counts)
    (gradient, probe_sums), unused = lax.scan(per_tile, (start_grad, start_probe), items)
    inside = gradient[:, :2 * TILE_SIDE, :grid_cols * TILE_SIDE]
    updated = image + inside[:2] / (inside[2] + object_damp)
    object_new = updated.reshape(2, 2, TILE_SIDE, grid_cols, TILE_SIDE).transpose(1, 3, 0, 2, 4)
    object_new = object_new.reshape(TILES, 2, TILE_SIDE, TILE_SIDE)
    probe_step = probe_sums[:2] / (probe_sums[2] + probe_damp)
    return (object_new, probe_step)
```

```python
import functools
import math

import jax
import jax.numpy as jnp
from jax import lax
from jax.experimental import pallas as pl
from jax.experimental.pallas import tpu as pltpu
from jax.sharding import PartitionSpec as P

floor_amp = 0.5
object_damp = 0.5
probe_damp = 1.0
LANE = 128
CHUNK = 32


def passed_along(value, axis, steps):
    count = lax.axis_size(axis)
    first, last = (max(0, -steps), min(count, count - steps))
    return lax.ppermute(value, axis, [(source, source + steps) for source in range(first, last)])


def dft_tables(window):
    steps = jnp.arange(window, dtype=jnp.int32)
    phase = steps[:, None] * steps[None, :] % window
    angle = phase.astype(jnp.float32) * (2.0 * math.pi / window)
    scale = 1.0 / math.sqrt(window)
    return (
        (jnp.cos(angle) * scale).astype(jnp.bfloat16),
        (-jnp.sin(angle) * scale).astype(jnp.bfloat16),
    )


def scatter_block(acc, ch, k0, row, size, q, shift, keep):
    turned = [pltpu.roll(v, shift, 1) for v in q]
    count = len(q)
    for b in range(count + 1):
        if b == 0:
            value = jnp.where(keep, turned[0], 0.0)
        elif b == count:
            value = jnp.where(keep, 0.0, turned[count - 1])
        else:
            value = jnp.where(keep, turned[b], turned[b - 1])
        at = (ch, k0 + b, pl.ds(row, size), slice(None))
        acc[at] = acc[at] + value


def pattern_kernel(plan, window, row_base, low, high, n_part, *refs):
    offs, cnt, probe, tab_a, tab_b = refs[:5]
    intensity = refs[5]
    parts = refs[6 : 6 + n_part]
    out, sums = refs[6 + n_part : 8 + n_part]
    ext, acc, win, xb, hb, big, sem_in, sem_out, sem_int, ibuf = refs[8 + n_part :]
    blocks = window // LANE
    copies = []
    for i, (which, rows, cols, to_row, to_col) in enumerate(plan):
        for k in range((cols[1] - cols[0]) // LANE):
            copies.append(
                pltpu.make_async_copy(
                    parts[which].at[:, pl.ds(rows[0], rows[1] - rows[0]), pl.ds(cols[0] + k * LANE, LANE)],
                    ext.at[:, to_col // LANE + k, pl.ds(to_row, rows[1] - rows[0]), :],
                    sem_in.at[len(copies)],
                )
            )
    for copy in copies:
        copy.start()
    get_int = pltpu.make_async_copy(intensity, ibuf, sem_int)
    get_int.start()
    acc[...] = jnp.zeros(acc.shape, jnp.float32)
    sums[...] = jnp.zeros(sums.shape, jnp.float32)
    for copy in copies:
        copy.wait()
    get_int.wait()
    lane = lax.broadcasted_iota(jnp.int32, (CHUNK, LANE), 1)

    def step(slot, carry):
        row = offs[slot, 0]
        col = offs[slot, 1]

        @pl.when((row >= low) & (row < high))
        def _():
            base = row - row_base
            k0 = col // LANE
            shift = col % LANE
            back = lax.rem(LANE - shift, LANE)
            take = lane < LANE - shift
            keep = lane >= shift

            for i in range(0, window, CHUNK):
                got = []
                for ch in range(2):
                    turned = [
                        pltpu.roll(ext[ch, k0 + b, pl.ds(base + i, CHUNK), :], back, 1)
                        for b in range(blocks + 1)
                    ]
                    got.append(
                        [jnp.where(take, turned[b], turned[b + 1]) for b in range(blocks)]
                    )
                for b in range(blocks):
                    at = (slice(i, i + CHUNK), slice(b * LANE, (b + 1) * LANE))
                    wr, wi = got[0][b], got[1][b]
                    pr, pi = probe[(0,) + at], probe[(1,) + at]
                    win[(0,) + at] = wr
                    win[(1,) + at] = wi
                    sums[(2,) + at] += wr * wr + wi * wi
                    xb[at] = (pr * wr - pi * wi).astype(jnp.bfloat16)
                    xb[slice(window + i, window + i + CHUNK), at[1]] = (pr * wi + pi * wr).astype(
                        jnp.bfloat16
                    )
            half = jnp.dot(tab_a[...], xb[...], preferred_element_type=jnp.float32)
            hb[:, :window] = half[:window].astype(jnp.bfloat16)
            hb[:, window:] = half[window:].astype(jnp.bfloat16)
            big[...] = jnp.dot(hb[...], tab_b[...], preferred_element_type=jnp.float32)
            for i in range(0, window, CHUNK):
                re = big[i : i + CHUNK, :window]
                im = big[i : i + CHUNK, window:]
                power = jnp.maximum(re * re + im * im, floor_amp * floor_amp)
                seen = ibuf[slot, i : i + CHUNK, :].astype(jnp.float32)
                factor = jnp.sqrt(seen) * lax.rsqrt(power) - 1.0
                xb[i : i + CHUNK, :] = (re * factor).astype(jnp.bfloat16)
                xb[window + i : window + i + CHUNK, :] = (im * factor).astype(jnp.bfloat16)
            half = jnp.dot(tab_b[...], xb[...], preferred_element_type=jnp.float32)
            hb[:, :window] = half[:window].astype(jnp.bfloat16)
            hb[:, window:] = half[window:].astype(jnp.bfloat16)
            big[...] = jnp.dot(hb[...], tab_a[...], preferred_element_type=jnp.float32)
            for i in range(0, window, CHUNK):
                g_re, g_im = [], []
                for b in range(blocks):
                    at = (slice(i, i + CHUNK), slice(b * LANE, (b + 1) * LANE))
                    cr = big[at]
                    ci = big[slice(i, i + CHUNK), window + b * LANE : window + (b + 1) * LANE]
                    pr, pi = probe[(0,) + at], probe[(1,) + at]
                    wr, wi = win[(0,) + at], win[(1,) + at]
                    g_re.append(pr * cr + pi * ci)
                    g_im.append(pr * ci - pi * cr)
                    sums[(0,) + at] += wr * cr + wi * ci
                    sums[(1,) + at] += wr * ci - wi * cr
                scatter_block(acc, 0, k0, base + i, CHUNK, g_re, shift, keep)
                scatter_block(acc, 1, k0, base + i, CHUNK, g_im, shift, keep)

        return carry

    lax.fori_loop(0, cnt[0], step, 0)
    ends = []
    for ch in range(2):
        for k in range(acc.shape[1]):
            ends.append(
                pltpu.make_async_copy(
                    acc.at[ch, k], out.at[ch, :, pl.ds(k * LANE, LANE)], sem_out.at[ch, k]
                )
            )
    for copy in ends:
        copy.start()
    for copy in ends:
        copy.wait()


def run_patterns(plan, parts, offsets, counts, probe, tab_a, tab_b, intensity, row_base, rows, low, high, width):
    window = probe.shape[1]
    slots = intensity.shape[0]
    n_copy = sum((c[1] - c[0]) // LANE for _, _, c, _, _ in plan)
    smem = pl.BlockSpec(memory_space=pltpu.SMEM)
    vmem = pl.BlockSpec(memory_space=pltpu.VMEM)
    anys = pl.BlockSpec(memory_space=pl.ANY)
    n_block = width // LANE
    return pl.pallas_call(
        functools.partial(pattern_kernel, plan, window, row_base, low, high, len(parts)),
        out_shape=(
            jax.ShapeDtypeStruct((2, rows, width), jnp.float32),
            jax.ShapeDtypeStruct((3, window, window), jnp.float32),
        ),
        in_specs=[smem, smem, vmem, vmem, vmem, anys] + [anys] * len(parts),
        out_specs=(anys, vmem),
        scratch_shapes=[
            pltpu.VMEM((2, n_block, rows, LANE), jnp.float32),
            pltpu.VMEM((2, n_block, rows, LANE), jnp.float32),
            pltpu.VMEM((2, window, window), jnp.float32),
            pltpu.VMEM((2 * window, window), jnp.bfloat16),
            pltpu.VMEM((window, 2 * window), jnp.bfloat16),
            pltpu.VMEM((window, 2 * window), jnp.float32),
            pltpu.SemaphoreType.DMA((n_copy,)),
            pltpu.SemaphoreType.DMA((2, n_block)),
            pltpu.SemaphoreType.DMA,
            pltpu.VMEM((slots, window, window), jnp.bfloat16),
        ],
        compiler_params=pltpu.CompilerParams(vmem_limit_bytes=44 << 20),
        cost_estimate=pl.CostEstimate(
            flops=slots * 16 * window**3, bytes_accessed=30 << 20, transcendentals=0
        ),
    )(offsets, counts, probe, tab_a, tab_b, intensity, *parts)


def weight_kernel(window, tile, offs, cnt, probe, out, acc, power, sem):
    blocks = window // LANE
    acc[...] = jnp.zeros(acc.shape, jnp.float32)
    power[...] = probe[0] * probe[0] + probe[1] * probe[1]
    lane = lax.broadcasted_iota(jnp.int32, (CHUNK, LANE), 1)
    slots = offs.shape[1]
    for source in range(4):
        down, across = source // 2, source % 2

        def step(slot, carry):
            row = offs[source, slot, 0] - down * tile + window
            col = offs[source, slot, 1] - across * tile + window

            @pl.when((row > 0) & (col > 0))
            def _():
                k0 = col // LANE
                shift = col % LANE
                keep = lane >= shift
                for i in range(0, window, CHUNK):
                    q = [power[i : i + CHUNK, b * LANE : (b + 1) * LANE] for b in range(blocks)]
                    scatter_block(acc, 0, k0, row + i, CHUNK, q, shift, keep)

            return carry

        lax.fori_loop(0, cnt[source, 0], step, 0)
    ends = [
        pltpu.make_async_copy(
            acc.at[0, blocks + k, pl.ds(window, tile), :], out.at[:, pl.ds(k * LANE, LANE)], sem.at[k]
        )
        for k in range(tile // LANE)
    ]
    for copy in ends:
        copy.start()
    for copy in ends:
        copy.wait()


def weights(offs, cnt, probe, tile):
    window = probe.shape[1]
    side = tile + 2 * window
    smem = pl.BlockSpec(memory_space=pltpu.SMEM)
    vmem = pl.BlockSpec(memory_space=pltpu.VMEM)
    return pl.pallas_call(
        functools.partial(weight_kernel, window, tile),
        out_shape=jax.ShapeDtypeStruct((tile, tile), jnp.float32),
        in_specs=[smem, smem, vmem],
        out_specs=pl.BlockSpec(memory_space=pl.ANY),
        scratch_shapes=[
            pltpu.VMEM((1, side // LANE, side, LANE), jnp.float32),
            pltpu.VMEM((window, window), jnp.float32),
            pltpu.SemaphoreType.DMA((tile // LANE,)),
        ],
        compiler_params=pltpu.CompilerParams(vmem_limit_bytes=16 << 20),
        cost_estimate=pl.CostEstimate(flops=8 << 30, bytes_accessed=20 << 20, transcendentals=0),
    )(offs, cnt, probe)


def on_device(object_tiles, probe, intensity, counts, offsets):
    window = probe.shape[1]
    tile = object_tiles.shape[2]
    grid_cols = lax.axis_size("tile") // 2
    grid_col = lax.axis_index("tile") % grid_cols
    right_ok = (grid_col != grid_cols - 1).astype(jnp.float32)
    left_ok = (grid_col != 0).astype(jnp.float32)
    left_ok_int = (grid_col != 0).astype(jnp.int32)
    object_tile = object_tiles[0]
    rim_a = passed_along(object_tile[:, :window, :window], "tile", -grid_cols)
    strip = passed_along(object_tile[:, :, :window], "tile", -1) * right_ok
    rim_b = passed_along(object_tile[:, :window, window:], "tile", -grid_cols)
    corner = passed_along(rim_a, "tile", -1) * right_ok
    where = jnp.concatenate([offsets.reshape(-1), counts])
    where_left = passed_along(where, "tile", 1) * left_ok_int
    pair = jnp.stack([where, where_left])
    pair_up = passed_along(pair, "tile", grid_cols)
    four = jnp.concatenate([pair, pair_up], axis=0)
    offs4 = four[:, :-1].reshape(4, -1, 2)
    cnt4 = four[:, -1:]

    table_re, table_im = dft_tables(window)
    tab_a = jnp.block([[table_re, -table_im], [table_im, table_re]])
    tab_b = jnp.block([[table_re, table_im], [-table_im, table_re]])
    cut = tile - window
    side = tile + window
    acc_1, sums_1 = run_patterns(
        ((0, (0, tile), (0, tile), 0, 0), (1, (0, tile), (0, window), 0, tile)),
        (object_tile, strip),
        offsets, counts, probe, tab_a, tab_b, intensity, 0, tile, 0, cut + 1, side,
    )
    weight = weights(offs4, cnt4, probe, tile)
    side_1 = passed_along(acc_1[:, :, tile:], "tile", 1)
    acc_2, sums_2 = run_patterns(
        (
            (0, (cut, tile), (0, tile), 0, 0),
            (1, (cut, tile), (0, window), 0, tile),
            (2, (0, window), (0, window), window, 0),
            (3, (0, window), (0, tile - window), window, window),
            (4, (0, window), (0, window), window, tile),
        ),
        (object_tile, strip, rim_a, rim_b, corner),
        offsets, counts, probe, tab_a, tab_b, intensity, cut, 2 * window, cut + 1, tile, side,
    )
    side_2 = passed_along(acc_2[:, :, tile:], "tile", 1) * left_ok
    lower_b = passed_along(acc_2[:, window:, window:tile], "tile", grid_cols)
    lower_a = passed_along(
        acc_2[:, window:, :window] + side_2[:, window:], "tile", grid_cols
    )
    totals = lax.psum(sums_1 + sums_2, "tile")
    probe_step = totals[:2] / (totals[2] + probe_damp)
    total = acc_1[:, :, :tile]
    total = total.at[:, cut:, :].add(acc_2[:, :window, :tile])
    total = total.at[:, :, :window].add(side_1 * left_ok)
    total = total.at[:, cut:, :window].add(side_2[:, :window])
    total = total.at[:, :window, :window].add(lower_a)
    total = total.at[:, :window, window:].add(lower_b)
    object_new = object_tile + total / (weight + object_damp)
    return (object_new[None], probe_step)


def solution(mesh):
    in_specs = (
        P(("groups", "tile"), None, None, None),
        P(),
        P(("groups", "tile"), None, None),
        P(("groups", "tile")),
        P(("groups", "tile"), None),
    )
    out_specs = (P(("groups", "tile"), None, None, None), P("groups", None, None))
    return jax.shard_map(
        on_device, mesh=mesh, in_specs=in_specs, out_specs=out_specs, check_vma=False
    )
```

```python
import functools
import math

import jax
import jax.numpy as jnp
from jax import lax
from jax.experimental import pallas as pl
from jax.experimental.pallas import tpu as pltpu
from jax.sharding import PartitionSpec as P

floor_amp = 0.5
object_damp = 0.5
probe_damp = 1.0
LANE = 128
CHUNK = 32


def passed_along(value, axis, down, across):
    count = lax.axis_size(axis)
    cols = count // 2
    pairs = []
    for source in range(count):
        row, col = source // cols + down, source % cols + across
        if 0 <= row < 2 and 0 <= col < cols:
            pairs.append((source, row * cols + col))
    return lax.ppermute(value, axis, pairs)


def dft_tables(window):
    steps = jnp.arange(window, dtype=jnp.int32)
    phase = steps[:, None] * steps[None, :] % window
    angle = phase.astype(jnp.float32) * (2.0 * math.pi / window)
    scale = 1.0 / math.sqrt(window)
    return (
        (jnp.cos(angle) * scale).astype(jnp.bfloat16),
        (-jnp.sin(angle) * scale).astype(jnp.bfloat16),
    )


def scatter_block(acc, ch, k0, row, size, q, shift, keep):
    turned = [pltpu.roll(v, shift, 1) for v in q]
    count = len(q)
    for b in range(count + 1):
        if b == 0:
            value = jnp.where(keep, turned[0], 0.0)
        elif b == count:
            value = jnp.where(keep, 0.0, turned[count - 1])
        else:
            value = jnp.where(keep, turned[b], turned[b - 1])
        at = (ch, k0 + b, pl.ds(row, size), slice(None))
        acc[at] = acc[at] + value


def pattern_kernel(plan, window, row_base, low, high, n_part, *refs):
    offs, cnt, probe, tab_a, tab_b, intensity, earlier = refs[:7]
    parts = refs[7 : 7 + n_part]
    out, sums, mark = refs[7 + n_part : 10 + n_part]
    ext, acc, win, xb, hb, big, sem_in, sem_out, sem_int, ibuf = refs[10 + n_part :]
    mark[0, 0] = jnp.float32(1.0)
    blocks = window // LANE
    copies = []
    for i, (which, rows, cols, to_row, to_col) in enumerate(plan):
        for k in range((cols[1] - cols[0]) // LANE):
            copies.append(
                pltpu.make_async_copy(
                    parts[which].at[:, pl.ds(rows[0], rows[1] - rows[0]), pl.ds(cols[0] + k * LANE, LANE)],
                    ext.at[:, to_col // LANE + k, pl.ds(to_row, rows[1] - rows[0]), :],
                    sem_in.at[len(copies)],
                )
            )
    for copy in copies:
        copy.start()
    get_int = pltpu.make_async_copy(intensity, ibuf, sem_int)
    get_int.start()
    acc[...] = jnp.zeros(acc.shape, jnp.float32)
    sums[...] = earlier[...]
    for copy in copies:
        copy.wait()
    get_int.wait()
    lane = lax.broadcasted_iota(jnp.int32, (CHUNK, LANE), 1)

    def step(slot, carry):
        row = offs[slot, 0]
        col = offs[slot, 1]

        @pl.when((row >= low) & (row < high))
        def _():
            base = row - row_base
            k0 = col // LANE
            shift = col % LANE
            back = lax.rem(LANE - shift, LANE)
            take = lane < LANE - shift
            keep = lane >= shift

            for i in range(0, window, CHUNK):
                got = []
                for ch in range(2):
                    turned = [
                        pltpu.roll(ext[ch, k0 + b, pl.ds(base + i, CHUNK), :], back, 1)
                        for b in range(blocks + 1)
                    ]
                    got.append(
                        [jnp.where(take, turned[b], turned[b + 1]) for b in range(blocks)]
                    )
                for b in range(blocks):
                    at = (slice(i, i + CHUNK), slice(b * LANE, (b + 1) * LANE))
                    wr, wi = got[0][b], got[1][b]
                    pr, pi = probe[(0,) + at], probe[(1,) + at]
                    win[(0,) + at] = wr
                    win[(1,) + at] = wi
                    sums[(2,) + at] += wr * wr + wi * wi
                    xb[at] = (pr * wr - pi * wi).astype(jnp.bfloat16)
                    xb[slice(window + i, window + i + CHUNK), at[1]] = (pr * wi + pi * wr).astype(
                        jnp.bfloat16
                    )
            half = jnp.dot(tab_a[...], xb[...], preferred_element_type=jnp.float32)
            hb[:, :window] = half[:window].astype(jnp.bfloat16)
            hb[:, window:] = half[window:].astype(jnp.bfloat16)
            big[...] = jnp.dot(hb[...], tab_b[...], preferred_element_type=jnp.float32)
            for i in range(0, window, CHUNK):
                re = big[i : i + CHUNK, :window]
                im = big[i : i + CHUNK, window:]
                power = jnp.maximum(re * re + im * im, floor_amp * floor_amp)
                seen = ibuf[slot, i : i + CHUNK, :].astype(jnp.float32)
                factor = jnp.sqrt(seen) * lax.rsqrt(power) - 1.0
                xb[i : i + CHUNK, :] = (re * factor).astype(jnp.bfloat16)
                xb[window + i : window + i + CHUNK, :] = (im * factor).astype(jnp.bfloat16)
            half = jnp.dot(tab_b[...], xb[...], preferred_element_type=jnp.float32)
            hb[:, :window] = half[:window].astype(jnp.bfloat16)
            hb[:, window:] = half[window:].astype(jnp.bfloat16)
            big[...] = jnp.dot(hb[...], tab_a[...], preferred_element_type=jnp.float32)
            for i in range(0, window, CHUNK):
                g_re, g_im = [], []
                for b in range(blocks):
                    at = (slice(i, i + CHUNK), slice(b * LANE, (b + 1) * LANE))
                    cr = big[at]
                    ci = big[slice(i, i + CHUNK), window + b * LANE : window + (b + 1) * LANE]
                    pr, pi = probe[(0,) + at], probe[(1,) + at]
                    wr, wi = win[(0,) + at], win[(1,) + at]
                    g_re.append(pr * cr + pi * ci)
                    g_im.append(pr * ci - pi * cr)
                    sums[(0,) + at] += wr * cr + wi * ci
                    sums[(1,) + at] += wr * ci - wi * cr
                scatter_block(acc, 0, k0, base + i, CHUNK, g_re, shift, keep)
                scatter_block(acc, 1, k0, base + i, CHUNK, g_im, shift, keep)

        return carry

    lax.fori_loop(0, cnt[0], step, 0)
    ends = []
    for ch in range(2):
        for k in range(acc.shape[1]):
            ends.append(
                pltpu.make_async_copy(
                    acc.at[ch, k], out.at[ch, :, pl.ds(k * LANE, LANE)], sem_out.at[ch, k]
                )
            )
    for copy in ends:
        copy.start()
    for copy in ends:
        copy.wait()


def run_patterns(plan, parts, offsets, counts, probe, tab_a, tab_b, intensity, earlier, row_base, rows, low, high, width):
    window = probe.shape[1]
    slots = intensity.shape[0]
    n_copy = sum((c[1] - c[0]) // LANE for _, _, c, _, _ in plan)
    smem = pl.BlockSpec(memory_space=pltpu.SMEM)
    vmem = pl.BlockSpec(memory_space=pltpu.VMEM)
    anys = pl.BlockSpec(memory_space=pl.ANY)
    n_block = width // LANE
    return pl.pallas_call(
        functools.partial(pattern_kernel, plan, window, row_base, low, high, len(parts)),
        out_shape=(
            jax.ShapeDtypeStruct((2, rows, width), jnp.float32),
            jax.ShapeDtypeStruct((3, window, window), jnp.float32),
            jax.ShapeDtypeStruct((1, 1), jnp.float32),
        ),
        in_specs=[smem, smem, vmem, vmem, vmem, anys, vmem] + [anys] * len(parts),
        out_specs=(anys, vmem, smem),
        scratch_shapes=[
            pltpu.VMEM((2, n_block, rows, LANE), jnp.float32),
            pltpu.VMEM((2, n_block, rows, LANE), jnp.float32),
            pltpu.VMEM((2, window, window), jnp.float32),
            pltpu.VMEM((2 * window, window), jnp.bfloat16),
            pltpu.VMEM((window, 2 * window), jnp.bfloat16),
            pltpu.VMEM((window, 2 * window), jnp.float32),
            pltpu.SemaphoreType.DMA((n_copy,)),
            pltpu.SemaphoreType.DMA((2, n_block)),
            pltpu.SemaphoreType.DMA,
            pltpu.VMEM((slots, window, window), jnp.bfloat16),
        ],
        compiler_params=pltpu.CompilerParams(vmem_limit_bytes=44 << 20),
        cost_estimate=pl.CostEstimate(
            flops=slots * 16 * window**3, bytes_accessed=30 << 20, transcendentals=0
        ),
    )(offsets, counts, probe, tab_a, tab_b, intensity, earlier, *parts)


def weight_kernel(window, tile, offs, cnt, probe, out, acc, power, sem):
    blocks = window // LANE
    acc[...] = jnp.zeros(acc.shape, jnp.float32)
    power[...] = probe[0] * probe[0] + probe[1] * probe[1]
    lane = lax.broadcasted_iota(jnp.int32, (CHUNK, LANE), 1)
    slots = offs.shape[1]
    for source in range(4):
        down, across = source // 2, source % 2

        def step(slot, carry):
            row = offs[source, slot, 0] - down * tile + window
            col = offs[source, slot, 1] - across * tile + window

            @pl.when((row > 0) & (col > 0))
            def _():
                k0 = col // LANE
                shift = col % LANE
                keep = lane >= shift
                for i in range(0, window, CHUNK):
                    q = [power[i : i + CHUNK, b * LANE : (b + 1) * LANE] for b in range(blocks)]
                    scatter_block(acc, 0, k0, row + i, CHUNK, q, shift, keep)

            return carry

        lax.fori_loop(0, cnt[source, 0], step, 0)
    ends = [
        pltpu.make_async_copy(
            acc.at[0, blocks + k, pl.ds(window, tile), :], out.at[:, pl.ds(k * LANE, LANE)], sem.at[k]
        )
        for k in range(tile // LANE)
    ]
    for copy in ends:
        copy.start()
    for copy in ends:
        copy.wait()


def weights(offs, cnt, probe, tile):
    window = probe.shape[1]
    side = tile + 2 * window
    smem = pl.BlockSpec(memory_space=pltpu.SMEM)
    vmem = pl.BlockSpec(memory_space=pltpu.VMEM)
    return pl.pallas_call(
        functools.partial(weight_kernel, window, tile),
        out_shape=jax.ShapeDtypeStruct((tile, tile), jnp.float32),
        in_specs=[smem, smem, vmem],
        out_specs=pl.BlockSpec(memory_space=pl.ANY),
        scratch_shapes=[
            pltpu.VMEM((1, side // LANE, side, LANE), jnp.float32),
            pltpu.VMEM((window, window), jnp.float32),
            pltpu.SemaphoreType.DMA((tile // LANE,)),
        ],
        compiler_params=pltpu.CompilerParams(vmem_limit_bytes=16 << 20),
        cost_estimate=pl.CostEstimate(flops=8 << 30, bytes_accessed=20 << 20, transcendentals=0),
    )(offs, cnt, probe)


def join_kernel(obj, acc_1, acc_2, side_1, side_2, weight, out):
    tile = obj.shape[2]
    window = side_1.shape[2]
    i = pl.program_id(0)
    last = (i == pl.num_programs(0) - 1).astype(jnp.float32)
    for r in range(0, window, CHUNK):
        rows = slice(r, r + CHUNK)
        scale = 1.0 / (weight[rows, :] + object_damp)
        for ch in range(2):
            left = acc_1[ch, rows, :window] + side_1[ch, rows, :]
            left += last * (acc_2[ch, rows, :window] + side_2[ch, rows, :])
            rest = acc_1[ch, rows, window:tile] + last * acc_2[ch, rows, window:tile]
            total = jnp.concatenate([left, rest], axis=1)
            out[ch, rows, :] = jnp.where(i == 0, total, obj[ch, rows, :] + total * scale)


def join(obj, acc_1, acc_2, side_1, side_2, weight):
    tile = obj.shape[1]
    window = side_1.shape[2]
    side = tile + window
    moving = lambda i: (0, i, 0)
    fixed = lambda i: (0, 0, 0)
    return pl.pallas_call(
        join_kernel,
        grid=(tile // window,),
        out_shape=jax.ShapeDtypeStruct(obj.shape, jnp.float32),
        in_specs=[
            pl.BlockSpec((2, window, tile), moving),
            pl.BlockSpec((2, window, side), moving),
            pl.BlockSpec((2, window, side), fixed),
            pl.BlockSpec((2, window, window), moving),
            pl.BlockSpec((2, window, window), fixed),
            pl.BlockSpec((window, tile), lambda i: (i, 0)),
        ],
        out_specs=pl.BlockSpec((2, window, tile), moving),
        compiler_params=pltpu.CompilerParams(vmem_limit_bytes=40 << 20),
        cost_estimate=pl.CostEstimate(flops=8 << 20, bytes_accessed=22 << 20, transcendentals=0),
    )(obj, acc_1, acc_2, side_1, side_2, weight)


def finish_kernel(partial, obj, lower_a, lower_b, weight, totals, out, probe_step):
    window = lower_a.shape[1]
    for r in range(0, window, CHUNK):
        rows = slice(r, r + CHUNK)
        scale = 1.0 / (weight[rows, :] + object_damp)
        for ch in range(2):
            lower = jnp.concatenate([lower_a[ch, rows, :], lower_b[ch, rows, :]], axis=1)
            out[ch, rows, :] = obj[ch, rows, :] + (partial[ch, rows, :] + lower) * scale
        damped = 1.0 / (totals[2, rows, :] + probe_damp)
        for ch in range(2):
            probe_step[ch, rows, :] = totals[ch, rows, :] * damped


def finish(partial, obj, lower_a, lower_b, weight, totals):
    tile = obj.shape[1]
    window = lower_a.shape[1]
    fixed = lambda i: (0, 0, 0)
    strip = pl.BlockSpec((2, window, tile), fixed)
    return pl.pallas_call(
        finish_kernel,
        grid=(1,),
        out_shape=(
            jax.ShapeDtypeStruct(obj.shape, jnp.float32),
            jax.ShapeDtypeStruct((2, window, window), jnp.float32),
        ),
        in_specs=[
            strip,
            strip,
            pl.BlockSpec(lower_a.shape, fixed),
            pl.BlockSpec(lower_b.shape, fixed),
            pl.BlockSpec((window, tile), lambda i: (0, 0)),
            pl.BlockSpec(totals.shape, fixed),
        ],
        out_specs=(strip, pl.BlockSpec((2, window, window), fixed)),
        input_output_aliases={0: 0},
        compiler_params=pltpu.CompilerParams(vmem_limit_bytes=32 << 20),
        cost_estimate=pl.CostEstimate(flops=4 << 20, bytes_accessed=10 << 20, transcendentals=0),
    )(partial, obj, lower_a, lower_b, weight, totals)


def on_device(object_tiles, probe, intensity, counts, offsets):
    window = probe.shape[1]
    tile = object_tiles.shape[2]
    object_tile = object_tiles[0]
    strip = passed_along(object_tile[:, :, :window], "tile", 0, -1)
    rim_a = passed_along(object_tile[:, :window, :window], "tile", -1, 0)
    rim_b = passed_along(object_tile[:, :window, window:], "tile", -1, 0)
    where = jnp.concatenate([offsets.reshape(-1), counts])
    where_left = passed_along(where, "tile", 0, 1)
    pair = jnp.stack([where, where_left])
    pair_up = passed_along(pair, "tile", 1, 0)
    four = jnp.concatenate([pair, pair_up], axis=0)
    offs4 = four[:, :-1].reshape(4, -1, 2)
    cnt4 = four[:, -1:]

    table_re, table_im = dft_tables(window)
    tab_a = jnp.block([[table_re, -table_im], [table_im, table_re]])
    tab_b = jnp.block([[table_re, table_im], [-table_im, table_re]])
    cut = tile - window
    side = tile + window
    nothing = jnp.zeros((3, window, window), jnp.float32)
    acc_1, sums_1, mark = run_patterns(
        ((0, (0, tile), (0, tile), 0, 0), (1, (0, tile), (0, window), 0, tile)),
        (object_tile, strip),
        offsets, counts, probe, tab_a, tab_b, intensity, nothing, 0, tile, 0, cut + 1, side,
    )
    corner = passed_along(rim_a * mark[0, 0], "tile", 0, -1)
    side_1 = passed_along(acc_1[:, :, tile:], "tile", 0, 1)
    weight = weights(offs4, cnt4, probe, tile)
    acc_2, sums, _ = run_patterns(
        (
            (0, (cut, tile), (0, tile), 0, 0),
            (1, (cut, tile), (0, window), 0, tile),
            (2, (0, window), (0, window), window, 0),
            (3, (0, window), (0, tile - window), window, window),
            (4, (0, window), (0, window), window, tile),
        ),
        (object_tile, strip, rim_a, rim_b, corner),
        offsets, counts, probe, tab_a, tab_b, intensity, sums_1, cut, 2 * window, cut + 1, tile, side,
    )
    side_2 = passed_along(acc_2[:, :, tile:], "tile", 0, 1)
    lower_b = passed_along(acc_2[:, window:, window:tile], "tile", 1, 0)
    totals = lax.psum(sums, "tile")
    lower_a = passed_along(acc_2[:, window:, :window] + side_2[:, window:], "tile", 1, 0)
    partial = join(object_tile, acc_1, acc_2, side_1, side_2, weight)
    object_new, probe_step = finish(partial, object_tile, lower_a, lower_b, weight, totals)
    return (object_new[None], probe_step)


def solution(mesh):
    in_specs = (
        P(("groups", "tile"), None, None, None),
        P(),
        P(("groups", "tile"), None, None),
        P(("groups", "tile")),
        P(("groups", "tile"), None),
    )
    out_specs = (P(("groups", "tile"), None, None, None), P("groups", None, None))
    return jax.shard_map(
        on_device, mesh=mesh, in_specs=in_specs, out_specs=out_specs, check_vma=False
    )
```

```python
import functools
import math

import jax
import jax.numpy as jnp
from jax import lax
from jax.experimental import pallas as pl
from jax.experimental.pallas import tpu as pltpu
from jax.sharding import PartitionSpec as P

floor_amp = 0.5
object_damp = 0.5
probe_damp = 1.0
LANE = 128
CHUNK = 32


def passed_along(value, axis, down, across):
    count = lax.axis_size(axis)
    cols = count // 2
    pairs = []
    for source in range(count):
        row, col = source // cols + down, source % cols + across
        if 0 <= row < 2 and 0 <= col < cols:
            pairs.append((source, row * cols + col))
    return lax.ppermute(value, axis, pairs)


def dft_tables(window):
    steps = jnp.arange(window, dtype=jnp.int32)
    phase = steps[:, None] * steps[None, :] % window
    angle = phase.astype(jnp.float32) * (2.0 * math.pi / window)
    scale = 1.0 / math.sqrt(window)
    return (
        (jnp.cos(angle) * scale).astype(jnp.bfloat16),
        (-jnp.sin(angle) * scale).astype(jnp.bfloat16),
    )


def scatter_block(acc, ch, k0, row, size, q, shift, keep):
    turned = [pltpu.roll(v, shift, 1) for v in q]
    count = len(q)
    for b in range(count + 1):
        if b == 0:
            value = jnp.where(keep, turned[0], 0.0)
        elif b == count:
            value = jnp.where(keep, 0.0, turned[count - 1])
        else:
            value = jnp.where(keep, turned[b], turned[b - 1])
        at = (ch, k0 + b, pl.ds(row, size), slice(None))
        acc[at] = acc[at] + value


def pattern_kernel(plan, window, row_base, low, high, n_part, *refs):
    offs, cnt, probe, tab_a, tab_b, intensity, earlier, _ = refs[:8]
    parts = refs[8 : 8 + n_part]
    out, sums, mark = refs[8 + n_part : 11 + n_part]
    ext, acc, win, xb, hb, big, sem_in, sem_out, sem_int, ibuf = refs[11 + n_part :]
    mark[0, 0] = jnp.float32(1.0)
    blocks = window // LANE
    copies = []
    for i, (which, rows, cols, to_row, to_col) in enumerate(plan):
        for k in range((cols[1] - cols[0]) // LANE):
            copies.append(
                pltpu.make_async_copy(
                    parts[which].at[:, pl.ds(rows[0], rows[1] - rows[0]), pl.ds(cols[0] + k * LANE, LANE)],
                    ext.at[:, to_col // LANE + k, pl.ds(to_row, rows[1] - rows[0]), :],
                    sem_in.at[len(copies)],
                )
            )
    for copy in copies:
        copy.start()
    get_int = pltpu.make_async_copy(intensity, ibuf, sem_int)
    get_int.start()
    acc[...] = jnp.zeros(acc.shape, jnp.float32)
    sums[...] = earlier[...]
    for copy in copies:
        copy.wait()
    get_int.wait()
    lane = lax.broadcasted_iota(jnp.int32, (CHUNK, LANE), 1)

    def step(slot, carry):
        row = offs[slot, 0]
        col = offs[slot, 1]

        @pl.when((row >= low) & (row < high))
        def _():
            base = row - row_base
            k0 = col // LANE
            shift = col % LANE
            back = lax.rem(LANE - shift, LANE)
            take = lane < LANE - shift
            keep = lane >= shift

            for i in range(0, window, CHUNK):
                got = []
                for ch in range(2):
                    turned = [
                        pltpu.roll(ext[ch, k0 + b, pl.ds(base + i, CHUNK), :], back, 1)
                        for b in range(blocks + 1)
                    ]
                    got.append(
                        [jnp.where(take, turned[b], turned[b + 1]) for b in range(blocks)]
                    )
                for b in range(blocks):
                    at = (slice(i, i + CHUNK), slice(b * LANE, (b + 1) * LANE))
                    wr, wi = got[0][b], got[1][b]
                    pr, pi = probe[(0,) + at], probe[(1,) + at]
                    win[(0,) + at] = wr
                    win[(1,) + at] = wi
                    sums[(2,) + at] += wr * wr + wi * wi
                    xb[at] = (pr * wr - pi * wi).astype(jnp.bfloat16)
                    xb[slice(window + i, window + i + CHUNK), at[1]] = (pr * wi + pi * wr).astype(
                        jnp.bfloat16
                    )
            half = jnp.dot(tab_a[...], xb[...], preferred_element_type=jnp.float32)
            hb[:, :window] = half[:window].astype(jnp.bfloat16)
            hb[:, window:] = half[window:].astype(jnp.bfloat16)
            big[...] = jnp.dot(hb[...], tab_b[...], preferred_element_type=jnp.float32)
            for i in range(0, window, CHUNK):
                re = big[i : i + CHUNK, :window]
                im = big[i : i + CHUNK, window:]
                power = jnp.maximum(re * re + im * im, floor_amp * floor_amp)
                seen = ibuf[slot, i : i + CHUNK, :].astype(jnp.float32)
                factor = jnp.sqrt(seen) * lax.rsqrt(power) - 1.0
                xb[i : i + CHUNK, :] = (re * factor).astype(jnp.bfloat16)
                xb[window + i : window + i + CHUNK, :] = (im * factor).astype(jnp.bfloat16)
            half = jnp.dot(tab_b[...], xb[...], preferred_element_type=jnp.float32)
            hb[:, :window] = half[:window].astype(jnp.bfloat16)
            hb[:, window:] = half[window:].astype(jnp.bfloat16)
            big[...] = jnp.dot(hb[...], tab_a[...], preferred_element_type=jnp.float32)
            for i in range(0, window, CHUNK):
                g_re, g_im = [], []
                for b in range(blocks):
                    at = (slice(i, i + CHUNK), slice(b * LANE, (b + 1) * LANE))
                    cr = big[at]
                    ci = big[slice(i, i + CHUNK), window + b * LANE : window + (b + 1) * LANE]
                    pr, pi = probe[(0,) + at], probe[(1,) + at]
                    wr, wi = win[(0,) + at], win[(1,) + at]
                    g_re.append(pr * cr + pi * ci)
                    g_im.append(pr * ci - pi * cr)
                    sums[(0,) + at] += wr * cr + wi * ci
                    sums[(1,) + at] += wr * ci - wi * cr
                scatter_block(acc, 0, k0, base + i, CHUNK, g_re, shift, keep)
                scatter_block(acc, 1, k0, base + i, CHUNK, g_im, shift, keep)

        return carry

    lax.fori_loop(0, cnt[0], step, 0)
    ends = []
    for ch in range(2):
        for k in range(acc.shape[1]):
            ends.append(
                pltpu.make_async_copy(
                    acc.at[ch, k], out.at[ch, :, pl.ds(k * LANE, LANE)], sem_out.at[ch, k]
                )
            )
    for copy in ends:
        copy.start()
    for copy in ends:
        copy.wait()


def run_patterns(plan, parts, offsets, counts, probe, tab_a, tab_b, intensity, earlier, after, row_base, rows, low, high, width):
    window = probe.shape[1]
    slots = intensity.shape[0]
    n_copy = sum((c[1] - c[0]) // LANE for _, _, c, _, _ in plan)
    smem = pl.BlockSpec(memory_space=pltpu.SMEM)
    vmem = pl.BlockSpec(memory_space=pltpu.VMEM)
    anys = pl.BlockSpec(memory_space=pl.ANY)
    n_block = width // LANE
    return pl.pallas_call(
        functools.partial(pattern_kernel, plan, window, row_base, low, high, len(parts)),
        out_shape=(
            jax.ShapeDtypeStruct((2, rows, width), jnp.float32),
            jax.ShapeDtypeStruct((3, window, window), jnp.float32),
            jax.ShapeDtypeStruct((1, 1), jnp.float32),
        ),
        in_specs=[smem, smem, vmem, vmem, vmem, anys, vmem, smem] + [anys] * len(parts),
        out_specs=(anys, vmem, smem),
        scratch_shapes=[
            pltpu.VMEM((2, n_block, rows, LANE), jnp.float32),
            pltpu.VMEM((2, n_block, rows, LANE), jnp.float32),
            pltpu.VMEM((2, window, window), jnp.float32),
            pltpu.VMEM((2 * window, window), jnp.bfloat16),
            pltpu.VMEM((window, 2 * window), jnp.bfloat16),
            pltpu.VMEM((window, 2 * window), jnp.float32),
            pltpu.SemaphoreType.DMA((n_copy,)),
            pltpu.SemaphoreType.DMA((2, n_block)),
            pltpu.SemaphoreType.DMA,
            pltpu.VMEM((slots, window, window), jnp.bfloat16),
        ],
        compiler_params=pltpu.CompilerParams(vmem_limit_bytes=44 << 20),
        cost_estimate=pl.CostEstimate(
            flops=slots * 16 * window**3, bytes_accessed=30 << 20, transcendentals=0
        ),
    )(offsets, counts, probe, tab_a, tab_b, intensity, earlier, after, *parts)


def weight_kernel(window, tile, offs, cnt, probe, out, acc, power, sem):
    blocks = window // LANE
    acc[...] = jnp.zeros(acc.shape, jnp.float32)
    power[...] = probe[0] * probe[0] + probe[1] * probe[1]
    lane = lax.broadcasted_iota(jnp.int32, (CHUNK, LANE), 1)
    slots = offs.shape[1]
    for source in range(4):
        down, across = source // 2, source % 2

        def step(slot, carry):
            row = offs[source, slot, 0] - down * tile + window
            col = offs[source, slot, 1] - across * tile + window

            @pl.when((row > 0) & (col > 0))
            def _():
                k0 = col // LANE
                shift = col % LANE
                keep = lane >= shift
                for i in range(0, window, CHUNK):
                    q = [power[i : i + CHUNK, b * LANE : (b + 1) * LANE] for b in range(blocks)]
                    scatter_block(acc, 0, k0, row + i, CHUNK, q, shift, keep)

            return carry

        lax.fori_loop(0, cnt[source, 0], step, 0)
    ends = [
        pltpu.make_async_copy(
            acc.at[0, blocks + k, pl.ds(window, tile), :], out.at[:, pl.ds(k * LANE, LANE)], sem.at[k]
        )
        for k in range(tile // LANE)
    ]
    for copy in ends:
        copy.start()
    for copy in ends:
        copy.wait()


def weights(offs, cnt, probe, tile):
    window = probe.shape[1]
    side = tile + 2 * window
    smem = pl.BlockSpec(memory_space=pltpu.SMEM)
    vmem = pl.BlockSpec(memory_space=pltpu.VMEM)
    return pl.pallas_call(
        functools.partial(weight_kernel, window, tile),
        out_shape=jax.ShapeDtypeStruct((tile, tile), jnp.float32),
        in_specs=[smem, smem, vmem],
        out_specs=pl.BlockSpec(memory_space=pl.ANY),
        scratch_shapes=[
            pltpu.VMEM((1, side // LANE, side, LANE), jnp.float32),
            pltpu.VMEM((window, window), jnp.float32),
            pltpu.SemaphoreType.DMA((tile // LANE,)),
        ],
        compiler_params=pltpu.CompilerParams(vmem_limit_bytes=16 << 20),
        cost_estimate=pl.CostEstimate(flops=8 << 30, bytes_accessed=20 << 20, transcendentals=0),
    )(offs, cnt, probe)


def join_kernel(obj, acc_1, acc_2, side_1, side_2, weight, out):
    tile = obj.shape[2]
    window = side_1.shape[2]
    i = pl.program_id(0)
    last = (i == pl.num_programs(0) - 1).astype(jnp.float32)
    for r in range(0, window, CHUNK):
        rows = slice(r, r + CHUNK)
        scale = 1.0 / (weight[rows, :] + object_damp)
        for ch in range(2):
            left = acc_1[ch, rows, :window] + side_1[ch, rows, :]
            left += last * (acc_2[ch, rows, :window] + side_2[ch, rows, :])
            rest = acc_1[ch, rows, window:tile] + last * acc_2[ch, rows, window:tile]
            total = jnp.concatenate([left, rest], axis=1)
            out[ch, rows, :] = jnp.where(i == 0, total, obj[ch, rows, :] + total * scale)


def join(obj, acc_1, acc_2, side_1, side_2, weight):
    tile = obj.shape[1]
    window = side_1.shape[2]
    side = tile + window
    moving = lambda i: (0, i, 0)
    fixed = lambda i: (0, 0, 0)
    return pl.pallas_call(
        join_kernel,
        grid=(tile // window,),
        out_shape=jax.ShapeDtypeStruct(obj.shape, jnp.float32),
        in_specs=[
            pl.BlockSpec((2, window, tile), moving),
            pl.BlockSpec((2, window, side), moving),
            pl.BlockSpec((2, window, side), fixed),
            pl.BlockSpec((2, window, window), moving),
            pl.BlockSpec((2, window, window), fixed),
            pl.BlockSpec((window, tile), lambda i: (i, 0)),
        ],
        out_specs=pl.BlockSpec((2, window, tile), moving),
        compiler_params=pltpu.CompilerParams(vmem_limit_bytes=40 << 20),
        cost_estimate=pl.CostEstimate(flops=8 << 20, bytes_accessed=22 << 20, transcendentals=0),
    )(obj, acc_1, acc_2, side_1, side_2, weight)


def finish_kernel(partial, obj, lower_a, lower_b, weight, totals, out, probe_step):
    window = lower_a.shape[1]
    for r in range(0, window, CHUNK):
        rows = slice(r, r + CHUNK)
        scale = 1.0 / (weight[rows, :] + object_damp)
        for ch in range(2):
            lower = jnp.concatenate([lower_a[ch, rows, :], lower_b[ch, rows, :]], axis=1)
            out[ch, rows, :] = obj[ch, rows, :] + (partial[ch, rows, :] + lower) * scale
        damped = 1.0 / (totals[2, rows, :] + probe_damp)
        for ch in range(2):
            probe_step[ch, rows, :] = totals[ch, rows, :] * damped


def finish(partial, obj, lower_a, lower_b, weight, totals):
    tile = obj.shape[1]
    window = lower_a.shape[1]
    fixed = lambda i: (0, 0, 0)
    strip = pl.BlockSpec((2, window, tile), fixed)
    return pl.pallas_call(
        finish_kernel,
        grid=(1,),
        out_shape=(
            jax.ShapeDtypeStruct(obj.shape, jnp.float32),
            jax.ShapeDtypeStruct((2, window, window), jnp.float32),
        ),
        in_specs=[
            strip,
            strip,
            pl.BlockSpec(lower_a.shape, fixed),
            pl.BlockSpec(lower_b.shape, fixed),
            pl.BlockSpec((window, tile), lambda i: (0, 0)),
            pl.BlockSpec(totals.shape, fixed),
        ],
        out_specs=(strip, pl.BlockSpec((2, window, window), fixed)),
        input_output_aliases={0: 0},
        compiler_params=pltpu.CompilerParams(vmem_limit_bytes=32 << 20),
        cost_estimate=pl.CostEstimate(flops=4 << 20, bytes_accessed=10 << 20, transcendentals=0),
    )(partial, obj, lower_a, lower_b, weight, totals)


def on_device(object_tiles, probe, intensity, counts, offsets):
    window = probe.shape[1]
    tile = object_tiles.shape[2]
    object_tile = object_tiles[0]
    where = jnp.concatenate([offsets.reshape(-1), counts])
    four = jnp.stack(
        [
            where,
            passed_along(where, "tile", 0, 1),
            passed_along(where, "tile", 1, 0),
            passed_along(where, "tile", 1, 1),
        ]
    )
    offs4 = four[:, :-1].reshape(4, -1, 2)
    cnt4 = four[:, -1:]
    strip = passed_along(object_tile[:, :, :window], "tile", 0, -1)
    rim_a = passed_along(object_tile[:, :window, :window], "tile", -1, 0)
    rim_b = passed_along(object_tile[:, :window, window:], "tile", -1, 0)

    table_re, table_im = dft_tables(window)
    tab_a = jnp.block([[table_re, -table_im], [table_im, table_re]])
    tab_b = jnp.block([[table_re, table_im], [-table_im, table_re]])
    cut = tile - window
    side = tile + window
    nothing = jnp.zeros((3, window, window), jnp.float32)
    acc_1, sums_1, mark = run_patterns(
        ((0, (0, tile), (0, tile), 0, 0), (1, (0, tile), (0, window), 0, tile)),
        (object_tile, strip),
        offsets, counts, probe, tab_a, tab_b, intensity, nothing, cnt4, 0, tile, 0, cut + 1, side,
    )
    corner = passed_along(rim_a * mark[0, 0], "tile", 0, -1)
    side_1 = passed_along(acc_1[:, :, tile:], "tile", 0, 1)
    weight = weights(offs4, cnt4, probe, tile)
    acc_2, sums, _ = run_patterns(
        (
            (0, (cut, tile), (0, tile), 0, 0),
            (1, (cut, tile), (0, window), 0, tile),
            (2, (0, window), (0, window), window, 0),
            (3, (0, window), (0, tile - window), window, window),
            (4, (0, window), (0, window), window, tile),
        ),
        (object_tile, strip, rim_a, rim_b, corner),
        offsets, counts, probe, tab_a, tab_b, intensity, sums_1, cnt4, cut, 2 * window, cut + 1, tile, side,
    )
    below = passed_along(acc_2[:, window:, tile:], "tile", 0, 1)
    lower_b = passed_along(acc_2[:, window:, window:tile], "tile", 1, 0)
    totals = lax.psum(sums, "tile")
    lower_a = passed_along(acc_2[:, window:, :window] + below, "tile", 1, 0)
    side_2 = passed_along(acc_2[:, :window, tile:], "tile", 0, 1)
    partial = join(object_tile, acc_1, acc_2, side_1, side_2, weight)
    object_new, probe_step = finish(partial, object_tile, lower_a, lower_b, weight, totals)
    return (object_new[None], probe_step)


def solution(mesh):
    in_specs = (
        P(("groups", "tile"), None, None, None),
        P(),
        P(("groups", "tile"), None, None),
        P(("groups", "tile")),
        P(("groups", "tile"), None),
    )
    out_specs = (P(("groups", "tile"), None, None, None), P("groups", None, None))
    return jax.shard_map(
        on_device, mesh=mesh, in_specs=in_specs, out_specs=out_specs, check_vma=False
    )
```

```python
import functools
import math

import jax
import jax.numpy as jnp
from jax import lax
from jax.experimental import pallas as pl
from jax.experimental.pallas import tpu as pltpu
from jax.sharding import PartitionSpec as P

floor_amp = 0.5
object_damp = 0.5
probe_damp = 1.0
LANE = 128
CHUNK = 32


def passed_along(value, axis, down, across):
    count = lax.axis_size(axis)
    cols = count // 2
    pairs = []
    for source in range(count):
        row, col = source // cols + down, source % cols + across
        if 0 <= row < 2 and 0 <= col < cols:
            pairs.append((source, row * cols + col))
    return lax.ppermute(value, axis, pairs)


def summed(value, axis):
    count = lax.axis_size(axis)
    odd = lax.axis_index(axis) % 2 == 1
    rows = value.shape[1] // 2
    swap = [(source, source + 1 - 2 * (source % 2)) for source in range(count)]
    upper, lower = value[:, :rows], value[:, rows:]
    got = lax.ppermute(jnp.where(odd, upper, lower), axis, swap)
    half = jnp.where(odd, lower, upper) + got
    groups = [list(range(0, count, 2)), list(range(1, count, 2))]
    half = lax.psum(half, axis, axis_index_groups=groups)
    other = lax.ppermute(half, axis, swap)
    first, second = jnp.where(odd, other, half), jnp.where(odd, half, other)
    return jnp.concatenate([first, second], axis=1)


def dft_tables(window):
    steps = jnp.arange(window, dtype=jnp.int32)
    phase = steps[:, None] * steps[None, :] % window
    angle = phase.astype(jnp.float32) * (2.0 * math.pi / window)
    scale = 1.0 / math.sqrt(window)
    return (
        (jnp.cos(angle) * scale).astype(jnp.bfloat16),
        (-jnp.sin(angle) * scale).astype(jnp.bfloat16),
    )


def scatter_block(acc, ch, k0, row, size, q, shift, keep):
    turned = [pltpu.roll(v, shift, 1) for v in q]
    count = len(q)
    for b in range(count + 1):
        if b == 0:
            value = jnp.where(keep, turned[0], 0.0)
        elif b == count:
            value = jnp.where(keep, 0.0, turned[count - 1])
        else:
            value = jnp.where(keep, turned[b], turned[b - 1])
        at = (ch, k0 + b, pl.ds(row, size), slice(None))
        acc[at] = acc[at] + value


def pattern_kernel(plan, window, row_base, low, high, n_part, *refs):
    offs, cnt, probe, tab_a, tab_b, intensity, earlier, _ = refs[:8]
    parts = refs[8 : 8 + n_part]
    out, sums, mark = refs[8 + n_part : 11 + n_part]
    ext, acc, win, xb, hb, big, sem_in, sem_out, sem_int, ibuf = refs[11 + n_part :]
    mark[0, 0] = jnp.float32(1.0)
    blocks = window // LANE
    copies = []
    for i, (which, rows, cols, to_row, to_col) in enumerate(plan):
        for k in range((cols[1] - cols[0]) // LANE):
            copies.append(
                pltpu.make_async_copy(
                    parts[which].at[:, pl.ds(rows[0], rows[1] - rows[0]), pl.ds(cols[0] + k * LANE, LANE)],
                    ext.at[:, to_col // LANE + k, pl.ds(to_row, rows[1] - rows[0]), :],
                    sem_in.at[len(copies)],
                )
            )
    for copy in copies:
        copy.start()
    get_int = pltpu.make_async_copy(intensity, ibuf, sem_int)
    get_int.start()
    acc[...] = jnp.zeros(acc.shape, jnp.float32)
    sums[...] = earlier[...]
    for copy in copies:
        copy.wait()
    get_int.wait()
    lane = lax.broadcasted_iota(jnp.int32, (CHUNK, LANE), 1)

    def step(slot, carry):
        row = offs[slot, 0]
        col = offs[slot, 1]

        @pl.when((row >= low) & (row < high))
        def _():
            base = row - row_base
            k0 = col // LANE
            shift = col % LANE
            back = lax.rem(LANE - shift, LANE)
            take = lane < LANE - shift
            keep = lane >= shift

            for i in range(0, window, CHUNK):
                got = []
                for ch in range(2):
                    turned = [
                        pltpu.roll(ext[ch, k0 + b, pl.ds(base + i, CHUNK), :], back, 1)
                        for b in range(blocks + 1)
                    ]
                    got.append(
                        [jnp.where(take, turned[b], turned[b + 1]) for b in range(blocks)]
                    )
                for b in range(blocks):
                    at = (slice(i, i + CHUNK), slice(b * LANE, (b + 1) * LANE))
                    wr, wi = got[0][b], got[1][b]
                    pr, pi = probe[(0,) + at], probe[(1,) + at]
                    win[(0,) + at] = wr
                    win[(1,) + at] = wi
                    sums[(2,) + at] += wr * wr + wi * wi
                    xb[at] = (pr * wr - pi * wi).astype(jnp.bfloat16)
                    xb[slice(window + i, window + i + CHUNK), at[1]] = (pr * wi + pi * wr).astype(
                        jnp.bfloat16
                    )
            half = jnp.dot(tab_a[...], xb[...], preferred_element_type=jnp.float32)
            hb[:, :window] = half[:window].astype(jnp.bfloat16)
            hb[:, window:] = half[window:].astype(jnp.bfloat16)
            big[...] = jnp.dot(hb[...], tab_b[...], preferred_element_type=jnp.float32)
            for i in range(0, window, CHUNK):
                re = big[i : i + CHUNK, :window]
                im = big[i : i + CHUNK, window:]
                power = jnp.maximum(re * re + im * im, floor_amp * floor_amp)
                seen = ibuf[slot, i : i + CHUNK, :].astype(jnp.float32)
                factor = jnp.sqrt(seen) * lax.rsqrt(power) - 1.0
                xb[i : i + CHUNK, :] = (re * factor).astype(jnp.bfloat16)
                xb[window + i : window + i + CHUNK, :] = (im * factor).astype(jnp.bfloat16)
            half = jnp.dot(tab_b[...], xb[...], preferred_element_type=jnp.float32)
            hb[:, :window] = half[:window].astype(jnp.bfloat16)
            hb[:, window:] = half[window:].astype(jnp.bfloat16)
            big[...] = jnp.dot(hb[...], tab_a[...], preferred_element_type=jnp.float32)
            for i in range(0, window, CHUNK):
                g_re, g_im = [], []
                for b in range(blocks):
                    at = (slice(i, i + CHUNK), slice(b * LANE, (b + 1) * LANE))
                    cr = big[at]
                    ci = big[slice(i, i + CHUNK), window + b * LANE : window + (b + 1) * LANE]
                    pr, pi = probe[(0,) + at], probe[(1,) + at]
                    wr, wi = win[(0,) + at], win[(1,) + at]
                    g_re.append(pr * cr + pi * ci)
                    g_im.append(pr * ci - pi * cr)
                    sums[(0,) + at] += wr * cr + wi * ci
                    sums[(1,) + at] += wr * ci - wi * cr
                scatter_block(acc, 0, k0, base + i, CHUNK, g_re, shift, keep)
                scatter_block(acc, 1, k0, base + i, CHUNK, g_im, shift, keep)

        return carry

    lax.fori_loop(0, cnt[0], step, 0)
    ends = []
    for ch in range(2):
        for k in range(acc.shape[1]):
            ends.append(
                pltpu.make_async_copy(
                    acc.at[ch, k], out.at[ch, :, pl.ds(k * LANE, LANE)], sem_out.at[ch, k]
                )
            )
    for copy in ends:
        copy.start()
    for copy in ends:
        copy.wait()


def run_patterns(plan, parts, offsets, counts, probe, tab_a, tab_b, intensity, earlier, after, row_base, rows, low, high, width):
    window = probe.shape[1]
    slots = intensity.shape[0]
    n_copy = sum((c[1] - c[0]) // LANE for _, _, c, _, _ in plan)
    smem = pl.BlockSpec(memory_space=pltpu.SMEM)
    vmem = pl.BlockSpec(memory_space=pltpu.VMEM)
    anys = pl.BlockSpec(memory_space=pl.ANY)
    n_block = width // LANE
    return pl.pallas_call(
        functools.partial(pattern_kernel, plan, window, row_base, low, high, len(parts)),
        out_shape=(
            jax.ShapeDtypeStruct((2, rows, width), jnp.float32),
            jax.ShapeDtypeStruct((3, window, window), jnp.float32),
            jax.ShapeDtypeStruct((1, 1), jnp.float32),
        ),
        in_specs=[smem, smem, vmem, vmem, vmem, anys, vmem, smem] + [anys] * len(parts),
        out_specs=(anys, vmem, smem),
        scratch_shapes=[
            pltpu.VMEM((2, n_block, rows, LANE), jnp.float32),
            pltpu.VMEM((2, n_block, rows, LANE), jnp.float32),
            pltpu.VMEM((2, window, window), jnp.float32),
            pltpu.VMEM((2 * window, window), jnp.bfloat16),
            pltpu.VMEM((window, 2 * window), jnp.bfloat16),
            pltpu.VMEM((window, 2 * window), jnp.float32),
            pltpu.SemaphoreType.DMA((n_copy,)),
            pltpu.SemaphoreType.DMA((2, n_block)),
            pltpu.SemaphoreType.DMA,
            pltpu.VMEM((slots, window, window), jnp.bfloat16),
        ],
        compiler_params=pltpu.CompilerParams(vmem_limit_bytes=44 << 20),
        cost_estimate=pl.CostEstimate(
            flops=slots * 16 * window**3, bytes_accessed=30 << 20, transcendentals=0
        ),
    )(offsets, counts, probe, tab_a, tab_b, intensity, earlier, after, *parts)


def weight_kernel(window, tile, offs, cnt, probe, out, acc, power, sem):
    blocks = window // LANE
    acc[...] = jnp.zeros(acc.shape, jnp.float32)
    power[...] = probe[0] * probe[0] + probe[1] * probe[1]
    lane = lax.broadcasted_iota(jnp.int32, (CHUNK, LANE), 1)
    slots = offs.shape[1]
    for source in range(4):
        down, across = source // 2, source % 2

        def step(slot, carry):
            row = offs[source, slot, 0] - down * tile + window
            col = offs[source, slot, 1] - across * tile + window

            @pl.when((row > 0) & (col > 0))
            def _():
                k0 = col // LANE
                shift = col % LANE
                keep = lane >= shift
                for i in range(0, window, CHUNK):
                    q = [power[i : i + CHUNK, b * LANE : (b + 1) * LANE] for b in range(blocks)]
                    scatter_block(acc, 0, k0, row + i, CHUNK, q, shift, keep)

            return carry

        lax.fori_loop(0, cnt[source, 0], step, 0)
    ends = [
        pltpu.make_async_copy(
            acc.at[0, blocks + k, pl.ds(window, tile), :], out.at[:, pl.ds(k * LANE, LANE)], sem.at[k]
        )
        for k in range(tile // LANE)
    ]
    for copy in ends:
        copy.start()
    for copy in ends:
        copy.wait()


def weights(offs, cnt, probe, tile):
    window = probe.shape[1]
    side = tile + 2 * window
    smem = pl.BlockSpec(memory_space=pltpu.SMEM)
    vmem = pl.BlockSpec(memory_space=pltpu.VMEM)
    return pl.pallas_call(
        functools.partial(weight_kernel, window, tile),
        out_shape=jax.ShapeDtypeStruct((tile, tile), jnp.float32),
        in_specs=[smem, smem, vmem],
        out_specs=pl.BlockSpec(memory_space=pl.ANY),
        scratch_shapes=[
            pltpu.VMEM((1, side // LANE, side, LANE), jnp.float32),
            pltpu.VMEM((window, window), jnp.float32),
            pltpu.SemaphoreType.DMA((tile // LANE,)),
        ],
        compiler_params=pltpu.CompilerParams(vmem_limit_bytes=16 << 20),
        cost_estimate=pl.CostEstimate(flops=8 << 30, bytes_accessed=20 << 20, transcendentals=0),
    )(offs, cnt, probe)


def join_kernel(obj, acc_1, acc_2, side_1, side_2, weight, out):
    tile = obj.shape[2]
    window = side_1.shape[2]
    i = pl.program_id(0)
    last = (i == pl.num_programs(0) - 1).astype(jnp.float32)
    for r in range(0, window, CHUNK):
        rows = slice(r, r + CHUNK)
        scale = 1.0 / (weight[rows, :] + object_damp)
        for ch in range(2):
            left = acc_1[ch, rows, :window] + side_1[ch, rows, :]
            left += last * (acc_2[ch, rows, :window] + side_2[ch, rows, :])
            rest = acc_1[ch, rows, window:tile] + last * acc_2[ch, rows, window:tile]
            total = jnp.concatenate([left, rest], axis=1)
            out[ch, rows, :] = jnp.where(i == 0, total, obj[ch, rows, :] + total * scale)


def join(obj, acc_1, acc_2, side_1, side_2, weight):
    tile = obj.shape[1]
    window = side_1.shape[2]
    side = tile + window
    moving = lambda i: (0, i, 0)
    fixed = lambda i: (0, 0, 0)
    return pl.pallas_call(
        join_kernel,
        grid=(tile // window,),
        out_shape=jax.ShapeDtypeStruct(obj.shape, jnp.float32),
        in_specs=[
            pl.BlockSpec((2, window, tile), moving),
            pl.BlockSpec((2, window, side), moving),
            pl.BlockSpec((2, window, side), fixed),
            pl.BlockSpec((2, window, window), moving),
            pl.BlockSpec((2, window, window), fixed),
            pl.BlockSpec((window, tile), lambda i: (i, 0)),
        ],
        out_specs=pl.BlockSpec((2, window, tile), moving),
        compiler_params=pltpu.CompilerParams(vmem_limit_bytes=40 << 20),
        cost_estimate=pl.CostEstimate(flops=8 << 20, bytes_accessed=22 << 20, transcendentals=0),
    )(obj, acc_1, acc_2, side_1, side_2, weight)


def finish_kernel(partial, obj, lower_a, lower_b, weight, totals, out, probe_step):
    window = lower_a.shape[1]
    for r in range(0, window, CHUNK):
        rows = slice(r, r + CHUNK)
        scale = 1.0 / (weight[rows, :] + object_damp)
        for ch in range(2):
            lower = jnp.concatenate([lower_a[ch, rows, :], lower_b[ch, rows, :]], axis=1)
            out[ch, rows, :] = obj[ch, rows, :] + (partial[ch, rows, :] + lower) * scale
        damped = 1.0 / (totals[2, rows, :] + probe_damp)
        for ch in range(2):
            probe_step[ch, rows, :] = totals[ch, rows, :] * damped


def finish(partial, obj, lower_a, lower_b, weight, totals):
    tile = obj.shape[1]
    window = lower_a.shape[1]
    fixed = lambda i: (0, 0, 0)
    strip = pl.BlockSpec((2, window, tile), fixed)
    return pl.pallas_call(
        finish_kernel,
        grid=(1,),
        out_shape=(
            jax.ShapeDtypeStruct(obj.shape, jnp.float32),
            jax.ShapeDtypeStruct((2, window, window), jnp.float32),
        ),
        in_specs=[
            strip,
            strip,
            pl.BlockSpec(lower_a.shape, fixed),
            pl.BlockSpec(lower_b.shape, fixed),
            pl.BlockSpec((window, tile), lambda i: (0, 0)),
            pl.BlockSpec(totals.shape, fixed),
        ],
        out_specs=(strip, pl.BlockSpec((2, window, window), fixed)),
        input_output_aliases={0: 0},
        compiler_params=pltpu.CompilerParams(vmem_limit_bytes=32 << 20),
        cost_estimate=pl.CostEstimate(flops=4 << 20, bytes_accessed=10 << 20, transcendentals=0),
    )(partial, obj, lower_a, lower_b, weight, totals)


def on_device(object_tiles, probe, intensity, counts, offsets):
    window = probe.shape[1]
    tile = object_tiles.shape[2]
    object_tile = object_tiles[0]
    where = jnp.concatenate([offsets.reshape(-1), counts])
    four = jnp.stack(
        [
            where,
            passed_along(where, "tile", 0, 1),
            passed_along(where, "tile", 1, 0),
            passed_along(where, "tile", 1, 1),
        ]
    )
    offs4 = four[:, :-1].reshape(4, -1, 2)
    cnt4 = four[:, -1:]
    strip = passed_along(object_tile[:, :, :window], "tile", 0, -1)
    rim_a = passed_along(object_tile[:, :window, :window], "tile", -1, 0)
    rim_b = passed_along(object_tile[:, :window, window:], "tile", -1, 0)

    table_re, table_im = dft_tables(window)
    tab_a = jnp.block([[table_re, -table_im], [table_im, table_re]])
    tab_b = jnp.block([[table_re, table_im], [-table_im, table_re]])
    cut = tile - window
    side = tile + window
    nothing = jnp.zeros((3, window, window), jnp.float32)
    acc_1, sums_1, mark = run_patterns(
        ((0, (0, tile), (0, tile), 0, 0), (1, (0, tile), (0, window), 0, tile)),
        (object_tile, strip),
        offsets, counts, probe, tab_a, tab_b, intensity, nothing, cnt4, 0, tile, 0, cut + 1, side,
    )
    corner = passed_along(rim_a * mark[0, 0], "tile", 0, -1)
    side_1 = passed_along(acc_1[:, :, tile:], "tile", 0, 1)
    weight = weights(offs4, cnt4, probe, tile)
    acc_2, sums, _ = run_patterns(
        (
            (0, (cut, tile), (0, tile), 0, 0),
            (1, (cut, tile), (0, window), 0, tile),
            (2, (0, window), (0, window), window, 0),
            (3, (0, window), (0, tile - window), window, window),
            (4, (0, window), (0, window), window, tile),
        ),
        (object_tile, strip, rim_a, rim_b, corner),
        offsets, counts, probe, tab_a, tab_b, intensity, sums_1, cnt4, cut, 2 * window, cut + 1, tile, side,
    )
    below = passed_along(acc_2[:, window:, tile:], "tile", 0, 1)
    lower_b = passed_along(acc_2[:, window:, window:tile], "tile", 1, 0)
    totals = summed(sums, "tile")
    lower_a = passed_along(acc_2[:, window:, :window] + below, "tile", 1, 0)
    side_2 = passed_along(acc_2[:, :window, tile:], "tile", 0, 1)
    partial = join(object_tile, acc_1, acc_2, side_1, side_2, weight)
    object_new, probe_step = finish(partial, object_tile, lower_a, lower_b, weight, totals)
    return (object_new[None], probe_step)


def solution(mesh):
    in_specs = (
        P(("groups", "tile"), None, None, None),
        P(),
        P(("groups", "tile"), None, None),
        P(("groups", "tile")),
        P(("groups", "tile"), None),
    )
    out_specs = (P(("groups", "tile"), None, None, None), P("groups", None, None))
    return jax.shard_map(
        on_device, mesh=mesh, in_specs=in_specs, out_specs=out_specs, check_vma=False
    )
```
